32 devices in a mesh: groups: 2 (over x), rows: 16 (over z, y, core).
Axes of the slice: x: 2, y: 2, z: 4, core: 2. Of those that a mesh axis runs over, the one named last changes fastest.
Arguments:
- rhs: float32 [2, 65536], P(None, ('groups', 'rows')), parts along dimension 1
- geometry: float32 [6, 65536], P(None, ('groups', 'rows')), parts along dimension 1, as said below
- proxies: float32 [6, 32768], P(None, ('groups', 'rows')), parts along dimension 1, as said below
- basis_in: bfloat16 [512, 2, 64, 128], P(('groups', 'rows')), parts along dimension 0, may hold values from -0.5 to 0.5
- basis_out: bfloat16 [512, 2, 64, 128], P(('groups', 'rows')), parts along dimension 0, may hold values from -6 to 6
- far_tasks: int32 [2, 6144], P(None, ('groups', 'rows')), parts along dimension 1, may hold values from 0 to 255, as said below
- near_tiles: int32 [4, 512], P(None, ('groups', 'rows')), parts along dimension 1, may hold values from 0 to 255, as said below
Outputs:
- second_vector: float32 [2, 65536], P(None, ('groups', 'rows')), parts along dimension 1
- third_vector: float32 [2, 65536], P(None, ('groups', 'rows')), parts along dimension 1
- hessenberg: float32 [10], P('groups'), parts along dimension 0
The draws below stay inside these ranges and needn't reach their ends.
There are 2 independent parts, one for each index of `groups`. The reference program is written for one: setup_inputs(seed, part) draws one part's arguments, and reference() takes and returns one part's arrays. A program takes and returns all parts, laid end to end along the dimension named above; each array names one. Nothing has to cross between parts.
Inputs may be any that keep to these rules, and one draw needn't show every extreme that they name: `far_tasks`: each row cluster is the row of exactly 36, 12 or 6 blocks, for an eighth, three eighths and half of the clusters; the source b of a block with row a satisfies b = a + o modulo 256 with 16 < o < 240; each device holds 192 blocks, of which at most 36 have their row clusters on any one device, and some device holds exactly 36 such blocks for some device. `near_tiles`: tile 0 of cluster r is r itself; the others are distinct clusters r + o modulo 256 with 1 <= |o| <= 16. `geometry`: panels of cluster c lie around a point of a sphere of radius 6 that moves slowly with c; areas are positive. `proxies`: proxies of cluster c lie around the same point as its panels; weights are positive.
All inputs are finite; a program needn't handle non-finite values.
Results may differ from the reference program's by a relative error of at most 0.0055.
The reference program's roundings to bfloat16 on the way count: a program that leaves them out, or rounds other values in their place, can miss the bound.
Values may be sent and summed in bfloat16 or wider, within the bound.
A program may use at most 128 MiB of HBM per device.

```python
import math
import jax
import jax.numpy as jnp
from jax import lax

CL_DEV = 16
PAN = 128
RANK = 64
NEAR = 4
FAR_MEAN = 12
TASK_DEV = 192
NCL = 256
NPAN = 32768
TASKS = 3072
N_ROWS = 16


def sphere_points(count):
    index = jnp.arange(count, dtype=jnp.float32)
    height = 1.0 - 2.0 * (index + 0.5) / count
    polar = jnp.arccos(height)
    turn = jnp.sqrt(count * math.pi) * polar
    return 6.0 * jnp.stack([jnp.sin(polar) * jnp.cos(turn), jnp.sin(polar) * jnp.sin(turn), height])


def point_cloud(key, clusters, members, spread, low_weight, high_weight):
    keys = jax.random.split(key, 4)
    count = clusters * members
    where = jnp.repeat(sphere_points(clusters), members, axis=1)
    offset = spread * jax.random.normal(keys[0], (3, count), jnp.float32)
    polar = jax.random.uniform(keys[1], (1, count), jnp.float32, 0.0, math.pi)
    azimuth = jax.random.uniform(keys[2], (1, count), jnp.float32, -math.pi, math.pi)
    weight = jnp.exp(jax.random.uniform(keys[3], (1, count), jnp.float32, math.log(low_weight), math.log(high_weight)))
    return jnp.concatenate([where + offset, polar, azimuth, weight], 0)


def draw_geometry(key, part):
    key = jax.random.fold_in(key, 1)
    return point_cloud(key, NCL, PAN, 0.5, 0.02, 0.2)


def draw_proxies(key, part):
    key = jax.random.fold_in(key, 2)
    return point_cloud(key, NCL, RANK, 0.75, 0.05, 0.5)


def draw_rhs(key, part):
    key = jax.random.fold_in(key, 3)
    keys = jax.random.split(key, 2)
    ramp = jnp.arange(NPAN, dtype=jnp.float32)[None, :] / NPAN
    spread = 10.0 ** jax.random.uniform(keys[1], (2, NPAN), jnp.float32, 0.0, 1.0)
    base = jax.random.normal(keys[0], (2, NPAN), jnp.float32)
    scale = 1.0 + 2.0 * ramp
    return base * spread * scale


def draw_far_tasks(key, part):
    key = jax.random.fold_in(key, 4)
    keys = jax.random.split(key, 3)
    device_order = jax.random.permutation(keys[0], N_ROWS).astype(jnp.int32)
    owner = jnp.arange(NCL, dtype=jnp.int32) // CL_DEV
    heavy = device_order[owner] < N_ROWS // 8
    mixing = jax.random.permutation(keys[2], NCL).astype(jnp.int32)
    scores = jnp.where(heavy, 0, NCL) + mixing
    order = jnp.argsort(scores, stable=True).astype(jnp.int32)
    place = jnp.zeros((NCL,), jnp.int32).at[order].set(jnp.arange(NCL, dtype=jnp.int32))
    counts = jnp.where(place < NCL // 8, 3 * FAR_MEAN, jnp.where(place < NCL // 2, FAR_MEAN, FAR_MEAN // 2)).astype(jnp.int32)
    ends = jnp.cumsum(counts).astype(jnp.int32)
    slots = jnp.arange(TASKS, dtype=jnp.int32)
    task_rows = jnp.searchsorted(ends, slots, side='right').astype(jnp.int32)
    offsets = jax.random.randint(keys[1], (TASKS,), 0, NCL - 2 * CL_DEV - 1, jnp.int32)
    task_srcs = (task_rows + CL_DEV + 1 + offsets) % NCL
    spread_rows = jnp.transpose(task_rows.reshape(TASK_DEV, N_ROWS)).reshape(TASKS)
    spread_srcs = jnp.transpose(task_srcs.reshape(TASK_DEV, N_ROWS)).reshape(TASKS)
    return jnp.stack([spread_rows, spread_srcs]).astype(jnp.int32)


def draw_near_tiles(key, part):
    key = jax.random.fold_in(key, 5)
    width = 2 * CL_DEV
    scores = jax.random.randint(key, (NCL, width), 0, 1 << 20, jnp.int32) * width + jnp.arange(width, dtype=jnp.int32)[None, :]
    picks = jnp.argsort(scores, axis=1, stable=True)[:, :NEAR - 1].astype(jnp.int32)
    shifts = jnp.where(picks < CL_DEV, picks - CL_DEV, picks - CL_DEV + 1)
    own = jnp.arange(NCL, dtype=jnp.int32)[:, None]
    tiles = jnp.concatenate([own, (own + shifts) % NCL], 1)
    return jnp.transpose(tiles).astype(jnp.int32)


def levels(key, extent, shards, smallest, high):
    factor_of = 1.0
    for axis_at, parts in shards:
        steps = jax.random.uniform(jax.random.fold_in(jax.random.fold_in(key, 6), axis_at), (parts,), jnp.float32, smallest / len(shards), high / len(shards))
        factor_of = factor_of * jnp.repeat(jnp.exp(steps), extent[axis_at] // parts).reshape((-1,) + (1,) * (len(extent) - 1 - axis_at))
    return factor_of


def scatter_about(key, shape, scale, most, cuts=(), kind=jnp.bfloat16):
    gain = levels(key, shape, cuts, -0.22, 0.18) if cuts else 1.0
    values = jax.random.normal(key, shape, jnp.float32) * scale * gain
    return jnp.minimum(jnp.maximum(values, -most), most).astype(kind)


def setup_inputs(seed: int = 0, part: int = 0) -> dict:
    seeds = jax.random.split(jax.random.key(seed), 8)
    part_splits = jax.random.split(jax.random.fold_in(seeds[7], part), 8)
    return {
        "rhs": draw_rhs(jax.random.fold_in(jax.random.fold_in(seeds[7], part), 71), part),
        "geometry": draw_geometry(jax.random.fold_in(jax.random.fold_in(seeds[7], part), 71), part),
        "proxies": draw_proxies(jax.random.fold_in(jax.random.fold_in(seeds[7], part), 71), part),
        "basis_in": scatter_about(part_splits[3], (NCL, 2, RANK, PAN), PAN ** -0.5, 0.5, ((0, 16),)),
        "basis_out": scatter_about(part_splits[4], (NCL, 2, RANK, PAN), 1.0, 6.0, ((0, 16),)),
        "far_tasks": draw_far_tasks(jax.random.fold_in(jax.random.fold_in(seeds[7], part), 71), part),
        "near_tiles": draw_near_tiles(jax.random.fold_in(jax.random.fold_in(seeds[7], part), 71), part),
    }


coulomb = 1.0 / (4.0 * 3.141592653589793)
kappa = 0.5
ratio = 4.0
eps = 1e-06

def kernel_blocks(target, source):
    diff_x = target[0][:, None] - source[0][None, :]
    diff_y = target[1][:, None] - source[1][None, :]
    diff_z = target[2][:, None] - source[2][None, :]
    dist_sq = diff_x * diff_x + diff_y * diff_y + diff_z * diff_z + target[5][:, None] + source[5][None, :]
    radius = jnp.sqrt(dist_sq)
    inverse = 1.0 / radius
    cube = inverse * inverse * inverse
    screen = jnp.exp(-kappa * radius)
    growth = (1.0 + kappa * radius) * screen
    weight = source[5][None, :]
    src_nx = (jnp.sin(source[3]) * jnp.cos(source[4]))[None, :]
    src_ny = (jnp.sin(source[3]) * jnp.sin(source[4]))[None, :]
    src_nz = jnp.cos(source[3])[None, :]
    tgt_nx = (jnp.sin(target[3]) * jnp.cos(target[4]))[:, None]
    tgt_ny = (jnp.sin(target[3]) * jnp.sin(target[4]))[:, None]
    tgt_nz = jnp.cos(target[3])[:, None]
    single = coulomb * weight * inverse
    double = coulomb * weight * (diff_x * src_nx + diff_y * src_ny + diff_z * src_nz) * cube
    adjoint = -coulomb * weight * (diff_x * tgt_nx + diff_y * tgt_ny + diff_z * tgt_nz) * cube
    upper = jnp.stack([double - ratio * double * growth, single * screen - single], 1)
    lower = jnp.stack([adjoint - adjoint * growth, adjoint - adjoint * growth / ratio], 1)
    return jnp.stack([upper, lower], 0)

def near_field(geometry, near_tiles, density):
    geo = geometry.reshape(6, NCL, PAN)
    dens = density.reshape(2, NCL, PAN)

    def one_row(index):
        target = geo[:, index]
        total = jnp.zeros((2, PAN), jnp.float32)
        for tile in range(NEAR):
            source_id = near_tiles[tile, index]
            block = kernel_blocks(target, geo[:, source_id])
            total = total + jnp.einsum('kilj,lj->ki', block, dens[:, source_id], precision=lax.Precision.HIGHEST)
        return total
    out = lax.map(one_row, jnp.arange(NCL, dtype=jnp.int32))
    return jnp.transpose(out, (1, 0, 2)).reshape(2, NPAN)

def couplings(proxies, far_tasks):
    pro = proxies.reshape(6, NCL, RANK)
    task_rows = far_tasks[0].reshape(N_ROWS, TASK_DEV)
    task_srcs = far_tasks[1].reshape(N_ROWS, TASK_DEV)

    def one_block(pair):
        mats = jax.vmap(lambda a, b: kernel_blocks(pro[:, a], pro[:, b]))(pair[0], pair[1])
        return mats.reshape(TASK_DEV, 2 * RANK, 2 * RANK).astype(jnp.bfloat16)
    return lax.map(one_block, (task_rows, task_srcs)).reshape(TASKS, 2 * RANK, 2 * RANK)

def far_field(basis_in, basis_out, coupled, far_tasks, density):
    low = density.astype(jnp.bfloat16).reshape(2, NCL, PAN)
    moments = jnp.einsum('ckrp,kcp->ckr', basis_in.astype(jnp.float32), low.astype(jnp.float32))
    moments = moments.astype(jnp.bfloat16).reshape(NCL, 2 * RANK)
    picked = moments[far_tasks[1]].reshape(N_ROWS, TASK_DEV, 2 * RANK)
    blocks = coupled.reshape(N_ROWS, TASK_DEV, 2 * RANK, 2 * RANK)

    def apply_block(pair):
        return jnp.einsum('tab,tb->ta', pair[0].astype(jnp.float32), pair[1].astype(jnp.float32))
    terms = lax.map(apply_block, (blocks, picked)).reshape(TASKS, 2 * RANK)
    expansion = jax.ops.segment_sum(terms, far_tasks[0], num_segments=NCL)
    low_exp = expansion.astype(jnp.bfloat16).reshape(NCL, 2, RANK)
    far = jnp.einsum('ckrp,ckr->kcp', basis_out.astype(jnp.float32), low_exp.astype(jnp.float32))
    return far.reshape(2, NPAN)

def reference(rhs, geometry, proxies, basis_in, basis_out, far_tasks, near_tiles):
    coupled = couplings(proxies, far_tasks)
    entries = 2.0 * NPAN

    def operate(density):
        diag = jnp.stack([(1.0 + ratio) / 2.0 * density[0], (1.0 + 1.0 / ratio) / 2.0 * density[1]])
        near = near_field(geometry, near_tiles, density)
        far = far_field(basis_in, basis_out, coupled, far_tasks, density)
        return diag + near + far
    first = rhs / jnp.sqrt(jnp.sum(rhs * rhs) / entries + eps)
    image = operate(first)
    h11 = jnp.sum(first * image) / entries
    image = image - h11 * first
    h21 = jnp.sqrt(jnp.sum(image * image) / entries + eps)
    second_vector = image / h21
    image = operate(second_vector)
    h12 = jnp.sum(first * image) / entries
    h22 = jnp.sum(second_vector * image) / entries
    image = image - h12 * first - h22 * second_vector
    h32 = jnp.sqrt(jnp.sum(image * image) / entries + eps)
    third_vector = image / h32
    return (second_vector, third_vector, jnp.stack([h11, h21, h12, h22, h32]))
```

```python
import functools

import jax
import jax.numpy as jnp
from jax import lax
from jax.experimental import pallas as pl
from jax.experimental.pallas import tpu as pltpu
from jax.sharding import PartitionSpec as P

coulomb = 1.0 / (4.0 * 3.141592653589793)
kappa = 0.5
ratio = 4.0
eps = 1e-06
MESH = pl.DeviceIdType.MESH

PROXY, NORM, MOMENT, EXPAND, DOTS = 0, 1, 2, 4, 6


def features(points):
    polar, azimuth = points[3], points[4]
    return jnp.stack(
        [
            points[0],
            points[1],
            points[2],
            jnp.sin(polar) * jnp.cos(azimuth),
            jnp.sin(polar) * jnp.sin(azimuth),
            jnp.cos(polar),
            points[5],
            jnp.zeros_like(points[0]),
        ]
    )


def pair_terms(target, source):
    tcol = lambda c: target[:, c : c + 1]
    srow = lambda c: source[c : c + 1, :]
    dx, dy, dz = tcol(0) - srow(0), tcol(1) - srow(1), tcol(2) - srow(2)
    dist_sq = dx * dx + dy * dy + dz * dz + tcol(6) + srow(6)
    inverse = lax.rsqrt(dist_sq)
    radius = dist_sq * inverse
    screen = jnp.exp(-kappa * radius)
    growth = (1.0 + kappa * radius) * screen
    single = (coulomb * srow(6)) * inverse
    cube = single * (inverse * inverse)
    double = cube * (dx * srow(3) + dy * srow(4) + dz * srow(5))
    adjoint = -cube * (dx * tcol(3) + dy * tcol(4) + dz * tcol(5))
    return single, double, adjoint, screen, growth


def total(x):
    x = jnp.sum(jnp.sum(x, axis=0), axis=0, keepdims=True)
    return jnp.broadcast_to(jnp.sum(x, axis=1, keepdims=True), x.shape)


def pack(values):
    row = lax.broadcasted_iota(jnp.int32, (16, 128), 0)
    out = jnp.zeros((16, 128), jnp.float32)
    for index, value in enumerate(values):
        out = jnp.where(row == index, value, out)
    return out


def kernel(
    n,
    near_ref,
    task_ref,
    rhs_ref,
    geo_ref,
    geo_col_ref,
    proxy_ref,
    basis_in_ref,
    basis_out_ref,
    rows_ref,
    second_ref,
    third_ref,
    hess_ref,
    wide_geo,
    all_proxy,
    near_mats,
    coupled,
    wide_u,
    mom_all,
    terms,
    exp_send,
    exp_recv,
    dots_send,
    dots_recv,
    near_out,
    far_out,
    low_exp,
    send_sem,
    recv_sem,
    halo_send,
    halo_recv,
):
    clusters = geo_ref.shape[0]
    pairs = clusters // 2
    tasks = task_ref.shape[1]
    near_count = near_ref.shape[0]
    entries = 2.0 * clusters * 128 * n
    me = lax.axis_index("rows")
    right, left = lax.rem(me + 1, n), lax.rem(me + n - 1, n)
    peer_of = lambda k: lax.rem(me + k, n)

    barrier = pltpu.get_barrier_semaphore()

    def greet(k, carry):
        pl.semaphore_signal(barrier, inc=1, device_id={"rows": peer_of(k)}, device_id_type=MESH)
        return carry

    lax.fori_loop(1, n, greet, 0)
    pl.semaphore_wait(barrier, n - 1)

    def to_all(phase, src_of, dst):
        def copy(k):
            return pltpu.make_async_remote_copy(
                src_ref=src_of(peer_of(k)),
                dst_ref=dst,
                send_sem=send_sem.at[phase, k],
                recv_sem=recv_sem.at[phase, k],
                device_id={"rows": peer_of(k)},
                device_id_type=MESH,
            )

        def start(k, carry):
            copy(k).start()
            return carry

        def wait(k, carry):
            copy(k).wait()
            return carry

        return (
            lambda: lax.fori_loop(1, n, start, 0),
            lambda: lax.fori_loop(1, n, wait, 0),
        )

    def halo(phase, src, at):
        copies = [
            pltpu.make_async_remote_copy(
                src_ref=src,
                dst_ref=at(where),
                send_sem=halo_send.at[phase, side],
                recv_sem=halo_recv.at[phase, side],
                device_id={"rows": device},
                device_id_type=MESH,
            )
            for side, (where, device) in enumerate(((0, right), (2 * clusters, left)))
        ]

        def start():
            for copy in copies:
                copy.start()

        def wait():
            for copy in copies:
                copy.wait()

        return start, wait

    def dots_phase(index):
        return to_all(DOTS - 1 + index if index else NORM, lambda p: dots_send.at[index], dots_recv.at[index, me])

    rhs = rhs_ref[...]
    message = pack([total(rhs * rhs)])
    dots_send[0] = message
    norm_start, norm_wait = dots_phase(0)
    norm_start()
    dots_recv[0, me] = message
    geo_start, geo_wait = halo(0, geo_ref, lambda where: wide_geo.at[pl.ds(where, clusters)])
    geo_start()
    wide_geo[pl.ds(clusters, clusters)] = geo_ref[...]
    proxy_start, proxy_wait = to_all(PROXY, lambda p: proxy_ref, all_proxy.at[pl.ds(me * pairs, pairs)])
    proxy_start()
    all_proxy[pl.ds(me * pairs, pairs)] = proxy_ref[...]

    lane8 = lax.broadcasted_iota(jnp.int32, (8, 128), 1)
    row8 = lax.broadcasted_iota(jnp.int32, (8, 128), 0)
    own_row = (lane8 >= 64) == (row8 == 1)

    def send_density(step):
        def moment(c, carry):
            u0 = wide_u[step, 0, pl.ds(clusters + c, 1), :]
            u1 = wide_u[step, 1, pl.ds(clusters + c, 1), :]
            low = jnp.where(row8 == 0, u0, u1).astype(jnp.bfloat16)
            got = lax.dot_general(
                low, basis_in_ref[c], (((1,), (1,)), ((), ())), preferred_element_type=jnp.float32
            )
            got = jnp.where(lane8[:1] < 64, got[0:1], got[1:2])
            mom_all[step, pl.ds(me * clusters + c, 1), :] = got.astype(jnp.bfloat16).astype(jnp.float32)
            return carry

        u_start, u_wait = halo(
            1 + step,
            wide_u.at[step, :, pl.ds(clusters, clusters)],
            lambda where: wide_u.at[step, :, pl.ds(where, clusters)],
        )
        u_start()
        for c in range(clusters):
            moment(c, 0)
        own = mom_all.at[step, pl.ds(me * clusters, clusters)]
        mom_start, mom_wait = to_all(MOMENT + step, lambda p: own, own)
        mom_start()
        return u_wait, mom_wait

    def apply(step, u_wait, mom_wait):
        mom_wait()

        def far_terms(group, carry):
            for q in range(8):
                t = group * 8 + q
                picked = mom_all[step, pl.ds(task_ref[1, t], 1), :]
                low = jnp.broadcast_to(picked, (8, 128)).astype(jnp.bfloat16)
                got = lax.dot_general(
                    low, coupled[t], (((1,), (1,)), ((), ())), preferred_element_type=jnp.float32
                )
                terms[pl.ds(t, 1), :] = got[0:1]
            return carry

        lax.fori_loop(0, tasks // 8, far_terms, 0)
        term = terms[...]
        high = term.astype(jnp.bfloat16)
        rest = term - high.astype(jnp.float32)
        mid = rest.astype(jnp.bfloat16)
        low = (rest - mid.astype(jnp.float32)).astype(jnp.bfloat16)
        task_rows = rows_ref[0:1, :]
        width = task_rows.shape[1]

        def choose(block, carry):
            start = pl.multiple_of(block * 128, 128)
            wanted = start + lax.broadcasted_iota(jnp.int32, (128, width), 0)
            selector = jnp.where(task_rows == wanted, 1.0, 0.0).astype(jnp.bfloat16)
            dot = lambda part: jnp.dot(selector, part, preferred_element_type=jnp.float32)
            exp_send[step, pl.ds(start, 128), :] = dot(high) + (dot(mid) + dot(low))
            return carry

        lax.fori_loop(0, n * clusters // 128, choose, 0)
        exp_start, exp_wait = to_all(
            EXPAND + step,
            lambda p: exp_send.at[step, pl.ds(p * clusters, clusters)],
            exp_recv.at[step, me],
        )
        exp_start()
        exp_recv[step, me] = exp_send[step, pl.ds(me * clusters, clusters), :]
        u_wait()

        def near_apply(r, carry):
            acc = [jnp.zeros((128, 128), jnp.float32) for _ in range(2)]
            for t in range(near_count):
                b = near_ref[t, r]
                u0 = wide_u[step, 0, pl.ds(b, 1), :]
                u1 = wide_u[step, 1, pl.ds(b, 1), :]
                for k in range(2):
                    acc[k] = acc[k] + (
                        near_mats[r * near_count + t, k, :, 0:128] * u0
                        + near_mats[r * near_count + t, k, :, 128:256] * u1
                    )
            for k in range(2):
                near_out[k, pl.ds(r, 1), :] = jnp.sum(jnp.transpose(acc[k]), axis=0, keepdims=True)
            return carry

        lax.fori_loop(0, clusters, near_apply, 0)
        exp_wait()
        low_exp[...] = jnp.sum(exp_recv[step], axis=0)
        for c in range(clusters):
            row = jnp.where(own_row & (row8 < 2), low_exp[pl.ds(c, 1), :], 0.0).astype(jnp.bfloat16)
            got = jnp.dot(row, basis_out_ref[c], preferred_element_type=jnp.float32)
            far_out[0, pl.ds(c, 1), :] = got[0:1]
            far_out[1, pl.ds(c, 1), :] = got[1:2]
        u = wide_u[step, :, pl.ds(clusters, clusters), :]
        which = lax.broadcasted_iota(jnp.int32, u.shape, 0)
        diag = jnp.where(which == 0, (1.0 + ratio) / 2.0, (1.0 + 1.0 / ratio) / 2.0)
        return diag * u + near_out[...] + far_out[...]

    def safe(top, bottom):
        return jnp.where(bottom > 0.0, top / jnp.where(bottom > 0.0, bottom, 1.0), 0.0)

    def exchange(index, values):
        message = pack(values)
        dots_send[index] = message
        start, wait = dots_phase(index)
        start()
        dots_recv[index, me] = message
        wait()
        return [dots_recv[index, :, q, :] for q in range(len(values))]

    add = lambda x: jnp.sum(x, axis=0, keepdims=True)

    norm_wait()
    rhs_sq = add(dots_recv[0, :, 0, :])
    first = rhs / jnp.sqrt(rhs_sq / entries + eps)
    wide_u[0, :, pl.ds(clusters, clusters), :] = first
    u_wait, mom_wait = send_density(0)

    geo_wait()

    def near_build(r, carry):
        for t in range(near_count):
            source = wide_geo[near_ref[t, r]]
            for lo in range(0, 128, 32):
                single, double, adjoint, screen, growth = pair_terms(geo_col_ref[r, lo : lo + 32, :], source)
                at = r * near_count + t
                near_mats[at, 0, lo : lo + 32, 0:128] = double - double * (ratio * growth)
                near_mats[at, 0, lo : lo + 32, 128:256] = single * screen - single
                near_mats[at, 1, lo : lo + 32, 0:128] = adjoint - adjoint * growth
                near_mats[at, 1, lo : lo + 32, 128:256] = adjoint - adjoint * (growth / ratio)
        return carry

    lax.fori_loop(0, clusters, near_build, 0)

    proxy_wait()
    terms[...] = jnp.zeros_like(terms)
    upper = lane8 >= 64
    part = jnp.where(upper[:1], 1.0 / ratio, 1.0)

    def cluster_points(c):
        both = all_proxy[lax.div(c, 2)]
        return jnp.where(upper.astype(jnp.int32) == lax.rem(c, 2), both, pltpu.roll(both, 64, 1))

    def far_build(group, carry):
        for q in range(2):
            t = group * 2 + q
            target = jnp.transpose(cluster_points(task_ref[0, t]))
            source = cluster_points(task_ref[1, t])
            for lo in range(0, 64, 32):
                single, double, adjoint, screen, growth = pair_terms(target[lo : lo + 32], source)
                top = jnp.where(
                    upper[:1], single * screen - single, double - double * (ratio * growth)
                )
                bottom = adjoint - adjoint * (growth * part)
                coupled[t, lo : lo + 32, :] = top.astype(jnp.bfloat16)
                coupled[t, 64 + lo : 96 + lo, :] = bottom.astype(jnp.bfloat16)
        return carry

    lax.fori_loop(0, tasks // 2, far_build, 0)

    image = apply(0, u_wait, mom_wait)
    ff, fw = total(first * first), total(first * image)
    c1 = safe(fw, ff)
    left_over = image - c1 * first
    ff, fw, c1, rr, fr = exchange(1, [ff, fw, c1, total(left_over * left_over), total(first * left_over)])
    h11 = add(fw) / entries
    d1 = c1 - h11
    h21 = jnp.sqrt(jnp.maximum(add(rr + 2.0 * d1 * fr + d1 * d1 * ff), 0.0) / entries + eps)
    second = (image - h11 * first) / h21
    second_ref[...] = second
    wide_u[1, :, pl.ds(clusters, clusters), :] = second
    u_wait, mom_wait = send_density(1)

    image = apply(1, u_wait, mom_wait)
    ff, fv, vv = total(first * first), total(first * second), total(second * second)
    fw, vw = total(first * image), total(second * image)
    c1 = safe(fw, ff)
    left_over = image - c1 * first
    c2 = safe(total(second * left_over), vv)
    left_over = left_over - c2 * second
    ff, fv, vv, fw, vw, c1, c2, rr, fr, vr = exchange(
        2,
        [ff, fv, vv, fw, vw, c1, c2]
        + [total(x * left_over) for x in (left_over, first, second)],
    )
    h12, h22 = add(fw) / entries, add(vw) / entries
    d1, d2 = c1 - h12, c2 - h22
    length_sq = add(rr + 2.0 * (d1 * fr + d2 * vr) + d1 * d1 * ff + 2.0 * d1 * d2 * fv + d2 * d2 * vv)
    h32 = jnp.sqrt(jnp.maximum(length_sq, 0.0) / entries + eps)
    third_ref[...] = (image - h12 * first - h22 * second) / h32
    out = jnp.zeros((8, 128), jnp.float32)
    for index, value in enumerate((h11, h21, h12, h22, h32)):
        out = jnp.where(lane8 == index, value, out)
    hess_ref[...] = out


def shards(rhs, geometry, proxies, basis_in, basis_out, far_tasks, near_tiles):
    clusters = basis_in.shape[0]
    rank = basis_in.shape[2]
    panels = geometry.shape[1]
    members = panels // clusters
    n = lax.axis_size("rows")
    total_clusters = clusters * n
    first_cluster = lax.axis_index("rows") * clusters
    near_local = (near_tiles - first_cluster + clusters) % total_clusters
    near_count = near_tiles.shape[0]
    tasks = far_tasks.shape[1]
    width = -(-tasks // 128) * 128

    geo = features(geometry).reshape(8, clusters, members)
    geo_row = jnp.transpose(geo, (1, 0, 2))
    geo_col = jnp.transpose(geo, (1, 2, 0))
    proxy = jnp.transpose(features(proxies).reshape(8, clusters // 2, 2 * rank), (1, 0, 2))
    task_rows = jnp.pad(far_tasks[0:1], ((0, 7), (0, width - tasks)), constant_values=-1)

    f32, bf16 = jnp.float32, jnp.bfloat16
    vmem = pl.BlockSpec(memory_space=pltpu.VMEM)
    smem = pl.BlockSpec(memory_space=pltpu.SMEM)
    second, third, hess = pl.pallas_call(
        functools.partial(kernel, n),
        out_shape=(
            jax.ShapeDtypeStruct((2, clusters, members), f32),
            jax.ShapeDtypeStruct((2, clusters, members), f32),
            jax.ShapeDtypeStruct((8, 128), f32),
        ),
        in_specs=[smem, smem] + [vmem] * 7,
        out_specs=(vmem, vmem, vmem),
        scratch_shapes=[
            pltpu.VMEM((3 * clusters, 8, members), f32),
            pltpu.VMEM((total_clusters // 2, 8, 2 * rank), f32),
            pltpu.VMEM((clusters * near_count, 2, members, 2 * members), f32),
            pltpu.VMEM((tasks, 2 * rank, 2 * rank), bf16),
            pltpu.VMEM((2, 2, 3 * clusters, members), f32),
            pltpu.VMEM((2, total_clusters, 2 * rank), f32),
            pltpu.VMEM((width, 2 * rank), f32),
            pltpu.VMEM((2, total_clusters, 2 * rank), f32),
            pltpu.VMEM((2, n, clusters, 2 * rank), f32),
            pltpu.VMEM((3, 16, 128), f32),
            pltpu.VMEM((3, n, 16, 128), f32),
            pltpu.VMEM((2, clusters, members), f32),
            pltpu.VMEM((2, clusters, members), f32),
            pltpu.VMEM((clusters, 2 * rank), f32),
            pltpu.SemaphoreType.DMA((8, n)),
            pltpu.SemaphoreType.DMA((8, n)),
            pltpu.SemaphoreType.DMA((3, 2)),
            pltpu.SemaphoreType.DMA((3, 2)),
        ],
        compiler_params=pltpu.CompilerParams(
            collective_id=0, has_side_effects=True, vmem_limit_bytes=48 * 1024 * 1024
        ),
    )(
        near_local,
        far_tasks,
        rhs.reshape(2, clusters, members),
        geo_row,
        geo_col,
        proxy,
        basis_in.reshape(clusters, 2 * rank, members),
        basis_out.reshape(clusters, 2 * rank, members),
        task_rows,
    )
    return (second.reshape(2, panels), third.reshape(2, panels), hess[0, :5])


def solution(mesh):
    return jax.shard_map(
        shards,
        mesh=mesh,
        in_specs=(
            P(None, ("groups", "rows")),
            P(None, ("groups", "rows")),
            P(None, ("groups", "rows")),
            P(("groups", "rows"), None, None, None),
            P(("groups", "rows"), None, None, None),
            P(None, ("groups", "rows")),
            P(None, ("groups", "rows")),
        ),
        out_specs=(P(None, ("groups", "rows")), P(None, ("groups", "rows")), P("groups")),
        check_vma=False,
    )
```

```python
import functools

import jax
import jax.numpy as jnp
from jax import lax
from jax.experimental import pallas as pl
from jax.experimental.pallas import tpu as pltpu
from jax.sharding import PartitionSpec as P

coulomb = 1.0 / (4.0 * 3.141592653589793)
kappa = 0.5
ratio = 4.0
eps = 1e-06
MESH = pl.DeviceIdType.MESH

FAR_UNROLL = 4
FAR_CHUNK = 32
NEAR_CHUNK = 32
TERM_UNROLL = 16
UNROLL = 1

PROXY, NORM, MOMENT, EXPAND, DOTS = 0, 1, 2, 4, 6


def features(points):
    polar, azimuth = points[3], points[4]
    return jnp.stack(
        [
            points[0],
            points[1],
            points[2],
            jnp.sin(polar) * jnp.cos(azimuth),
            jnp.sin(polar) * jnp.sin(azimuth),
            jnp.cos(polar),
            points[5],
            jnp.zeros_like(points[0]),
        ]
    )


def pair_terms(target, source):
    dx, dy, dz = target[0] - source[0], target[1] - source[1], target[2] - source[2]
    dist_sq = dx * dx + dy * dy + dz * dz + target[6] + source[6]
    inverse = lax.rsqrt(dist_sq)
    radius = dist_sq * inverse
    screen = jnp.exp(-kappa * radius)
    growth = (1.0 + kappa * radius) * screen
    single = (coulomb * source[6]) * inverse
    cube = single * (inverse * inverse)
    double = cube * (dx * source[3] + dy * source[4] + dz * source[5])
    adjoint = -cube * (dx * target[3] + dy * target[4] + dz * target[5])
    return single, double, adjoint, screen, growth


def total(x):
    x = jnp.sum(jnp.sum(x, axis=0), axis=0, keepdims=True)
    return jnp.broadcast_to(jnp.sum(x, axis=1, keepdims=True), x.shape)


def pack(values):
    row = lax.broadcasted_iota(jnp.int32, (16, 128), 0)
    out = jnp.zeros((16, 128), jnp.float32)
    for index, value in enumerate(values):
        out = jnp.where(row == index, value, out)
    return out


def kernel(
    n,
    near_ref,
    task_ref,
    rhs_ref,
    geo_ref,
    geo_col_ref,
    proxy_ref,
    basis_in_ref,
    basis_out_ref,
    rows_ref,
    second_ref,
    third_ref,
    hess_ref,
    wide_geo,
    all_proxy,
    near_mats,
    coupled,
    wide_u,
    mom_all,
    terms,
    exp_send,
    exp_recv,
    dots_send,
    dots_recv,
    near_out,
    far_out,
    pair_out,
    low_exp,
    spreader,
    send_sem,
    recv_sem,
    halo_send,
    halo_recv,
):
    clusters = geo_ref.shape[0]
    pairs = clusters // 2
    tasks = task_ref.shape[1]
    half = tasks // 2
    near_count = near_ref.shape[0]
    entries = 2.0 * clusters * 128 * n
    me = lax.axis_index("rows")
    right, left = lax.rem(me + 1, n), lax.rem(me + n - 1, n)
    peer_of = lambda k: lax.rem(me + k, n)

    barrier = pltpu.get_barrier_semaphore()

    def greet(k, carry):
        pl.semaphore_signal(barrier, inc=1, device_id={"rows": peer_of(k)}, device_id_type=MESH)
        return carry

    lax.fori_loop(1, n, greet, 0)
    pl.semaphore_wait(barrier, n - 1)

    def to_all(phase, src_of, dst):
        def copy(k):
            return pltpu.make_async_remote_copy(
                src_ref=src_of(peer_of(k)),
                dst_ref=dst,
                send_sem=send_sem.at[phase, k],
                recv_sem=recv_sem.at[phase, k],
                device_id={"rows": peer_of(k)},
                device_id_type=MESH,
            )

        def start(k, carry):
            copy(k).start()
            return carry

        def wait(k, carry):
            copy(k).wait()
            return carry

        return (
            lambda: lax.fori_loop(1, n, start, 0, unroll=UNROLL),
            lambda: lax.fori_loop(1, n, wait, 0, unroll=UNROLL),
        )

    def halo(phase, src, at):
        copies = [
            pltpu.make_async_remote_copy(
                src_ref=src,
                dst_ref=at(where),
                send_sem=halo_send.at[phase, side],
                recv_sem=halo_recv.at[phase, side],
                device_id={"rows": device},
                device_id_type=MESH,
            )
            for side, (where, device) in enumerate(((0, right), (2 * clusters, left)))
        ]

        def start():
            for copy in copies:
                copy.start()

        def wait():
            for copy in copies:
                copy.wait()

        return start, wait

    def dots_phase(index):
        return to_all(DOTS - 1 + index if index else NORM, lambda p: dots_send.at[index], dots_recv.at[index, me])

    rhs = rhs_ref[...]
    message = pack([total(rhs * rhs)])
    dots_send[0] = message
    norm_start, norm_wait = dots_phase(0)
    norm_start()
    dots_recv[0, me] = message
    geo_start, geo_wait = halo(0, geo_ref, lambda where: wide_geo.at[pl.ds(where, clusters)])
    geo_start()
    wide_geo[pl.ds(clusters, clusters)] = geo_ref[...]
    proxy_start, proxy_wait = to_all(PROXY, lambda p: proxy_ref, all_proxy.at[pl.ds(me * pairs, pairs)])
    proxy_start()
    all_proxy[pl.ds(me * pairs, pairs)] = proxy_ref[...]

    lane8 = lax.broadcasted_iota(jnp.int32, (8, 128), 1)
    row8 = lax.broadcasted_iota(jnp.int32, (8, 128), 0)
    upper = lane8 >= 64
    own_row = (lane8 >= 64) == (row8 == 1)

    def send_density(step):
        def moment(c, carry):
            u0 = wide_u[step, 0, pl.ds(clusters + c, 1), :]
            u1 = wide_u[step, 1, pl.ds(clusters + c, 1), :]
            low = jnp.where(row8 == 0, u0, u1).astype(jnp.bfloat16)
            got = lax.dot_general(
                low, basis_in_ref[c], (((1,), (1,)), ((), ())), preferred_element_type=jnp.float32
            )
            got = jnp.where(lane8[:1] < 64, got[0:1], got[1:2])
            mom_all[step, pl.ds(me * clusters + c, 1), :] = got.astype(jnp.bfloat16).astype(jnp.float32)
            return carry

        u_start, u_wait = halo(
            1 + step,
            wide_u.at[step, :, pl.ds(clusters, clusters)],
            lambda where: wide_u.at[step, :, pl.ds(where, clusters)],
        )
        u_start()
        for c in range(clusters):
            moment(c, 0)
        own = mom_all.at[step, pl.ds(me * clusters, clusters)]
        mom_start, mom_wait = to_all(MOMENT + step, lambda p: own, own)
        mom_start()
        return u_wait, mom_wait

    def apply(step, u_wait, mom_wait):
        mom_wait()

        def far_terms(group, carry):
            for q in range(TERM_UNROLL):
                p = group * TERM_UNROLL + q
                picked_a = mom_all[step, pl.ds(task_ref[1, p], 1), :]
                picked_b = mom_all[step, pl.ds(task_ref[1, half + p], 1), :]
                low = jnp.where(row8 == 0, picked_a, picked_b).astype(jnp.bfloat16)
                got = jnp.dot(low, coupled[p], preferred_element_type=jnp.float32)
                for k in range(2):
                    block = got[:, k * 128 : k * 128 + 128]
                    pair_out[k, pl.ds(p, 1), :] = jnp.where(upper[:1], block[1:2], block[0:1])
            return carry

        lax.fori_loop(0, half // TERM_UNROLL, far_terms, 0)
        out0, out1 = pair_out[0], pair_out[1]
        below = lax.broadcasted_iota(jnp.int32, out0.shape, 1) < 64
        terms[0:half, :] = jnp.where(below, out0, pltpu.roll(out1, 64, 1))
        terms[half:tasks, :] = jnp.where(below, pltpu.roll(out0, 64, 1), out1)
        term = terms[...]
        high = term.astype(jnp.bfloat16)
        rest = term - high.astype(jnp.float32)
        mid = rest.astype(jnp.bfloat16)
        low = (rest - mid.astype(jnp.float32)).astype(jnp.bfloat16)
        task_rows = rows_ref[0:1, :]
        width = task_rows.shape[1]

        def choose(block, carry):
            start = pl.multiple_of(block * 128, 128)
            wanted = start + lax.broadcasted_iota(jnp.int32, (128, width), 0)
            selector = jnp.where(task_rows == wanted, 1.0, 0.0).astype(jnp.bfloat16)
            dot = lambda part: jnp.dot(selector, part, preferred_element_type=jnp.float32)
            exp_send[step, pl.ds(start, 128), :] = dot(high) + (dot(mid) + dot(low))
            return carry

        lax.fori_loop(0, n * clusters // 128, choose, 0)
        exp_start, exp_wait = to_all(
            EXPAND + step,
            lambda p: exp_send.at[step, pl.ds(p * clusters, clusters)],
            exp_recv.at[step, me],
        )
        exp_start()
        exp_recv[step, me] = exp_send[step, pl.ds(me * clusters, clusters), :]
        u_wait()

        def near_apply(r, carry):
            acc = [jnp.zeros((128, 128), jnp.float32) for _ in range(2)]
            for t in range(near_count):
                b = near_ref[t, r]
                u0 = wide_u[step, 0, pl.ds(b, 1), :]
                u1 = wide_u[step, 1, pl.ds(b, 1), :]
                for k in range(2):
                    acc[k] = acc[k] + (
                        near_mats[r * near_count + t, k, :, 0:128] * u0
                        + near_mats[r * near_count + t, k, :, 128:256] * u1
                    )
            for k in range(2):
                near_out[k, pl.ds(r, 1), :] = jnp.sum(jnp.transpose(acc[k]), axis=0, keepdims=True)
            return carry

        lax.fori_loop(0, clusters, near_apply, 0)
        exp_wait()
        low_exp[...] = jnp.sum(exp_recv[step], axis=0)
        for c in range(clusters):
            row = jnp.where(own_row & (row8 < 2), low_exp[pl.ds(c, 1), :], 0.0).astype(jnp.bfloat16)
            got = jnp.dot(row, basis_out_ref[c], preferred_element_type=jnp.float32)
            far_out[0, pl.ds(c, 1), :] = got[0:1]
            far_out[1, pl.ds(c, 1), :] = got[1:2]
        u = wide_u[step, :, pl.ds(clusters, clusters), :]
        which = lax.broadcasted_iota(jnp.int32, u.shape, 0)
        diag = jnp.where(which == 0, (1.0 + ratio) / 2.0, (1.0 + 1.0 / ratio) / 2.0)
        return diag * u + near_out[...] + far_out[...]

    def safe(top, bottom):
        return jnp.where(bottom > 0.0, top / jnp.where(bottom > 0.0, bottom, 1.0), 0.0)

    def exchange(index, values):
        message = pack(values)
        dots_send[index] = message
        start, wait = dots_phase(index)
        start()
        dots_recv[index, me] = message
        wait()
        return [dots_recv[index, :, q, :] for q in range(len(values))]

    add = lambda x: jnp.sum(x, axis=0, keepdims=True)

    geo_wait()

    def near_build(r, carry):
        sources = [wide_geo[near_ref[t, r]] for t in range(near_count)]
        for lo in range(0, 128, NEAR_CHUNK):
            hi = lo + NEAR_CHUNK
            tcol = [
                jnp.broadcast_to(geo_col_ref[r, lo:hi, c : c + 1], (NEAR_CHUNK, 128)) for c in range(7)
            ]
            for t in range(near_count):
                srow = [sources[t][c : c + 1, :] for c in range(7)]
                single, double, adjoint, screen, growth = pair_terms(tcol, srow)
                at = r * near_count + t
                near_mats[at, 0, lo:hi, 0:128] = double - double * (ratio * growth)
                near_mats[at, 0, lo:hi, 128:256] = single * screen - single
                near_mats[at, 1, lo:hi, 0:128] = adjoint - adjoint * growth
                near_mats[at, 1, lo:hi, 128:256] = adjoint - adjoint * (growth / ratio)
        return carry

    lax.fori_loop(0, clusters, near_build, 0)

    norm_wait()
    rhs_sq = add(dots_recv[0, :, 0, :])
    first = rhs / jnp.sqrt(rhs_sq / entries + eps)
    wide_u[0, :, pl.ds(clusters, clusters), :] = first
    u_wait, mom_wait = send_density(0)

    proxy_wait()
    terms[...] = jnp.zeros_like(terms)
    row = lax.broadcasted_iota(jnp.int32, spreader.shape, 0)
    lane = lax.broadcasted_iota(jnp.int32, spreader.shape, 1)
    same = (row % 8 == lane // 128) & (row // 24 == (lane % 128) // 64)
    spreader[...] = jnp.where(same, 1.0, 0.0).astype(jnp.bfloat16)

    def cluster(c):
        both = all_proxy[lax.div(c, 2)]
        return jnp.where(lax.rem(c, 2) == 0, both, pltpu.roll(both, 64, 1))

    def split(x):
        high = x.astype(jnp.bfloat16).astype(jnp.float32)
        mid = (x - high).astype(jnp.bfloat16).astype(jnp.float32)
        return [high, mid, x - high - mid]

    def far_build(group, carry):
        for q in range(FAR_UNROLL):
            p = group * FAR_UNROLL + q
            target = jnp.where(
                upper, pltpu.roll(cluster(task_ref[0, half + p]), 64, 1), cluster(task_ref[0, p])
            )
            parts = split(cluster(task_ref[1, p])) + split(cluster(task_ref[1, half + p]))
            parts = jnp.transpose(jnp.concatenate(parts, axis=0))[0:64].astype(jnp.bfloat16)
            spread = jnp.dot(parts, spreader[...], preferred_element_type=jnp.float32)
            trow = [target[c : c + 1, :] for c in range(7)]
            for lo in range(0, 64, FAR_CHUNK):
                hi = lo + FAR_CHUNK
                scol = [spread[lo:hi, c * 128 : c * 128 + 128] for c in range(7)]
                single, double, adjoint, screen, growth = pair_terms(trow, scol)
                coupled[p, lo:hi, 0:128] = (double - double * (ratio * growth)).astype(jnp.bfloat16)
                coupled[p, 64 + lo : 64 + hi, 0:128] = (single * screen - single).astype(jnp.bfloat16)
                coupled[p, lo:hi, 128:256] = (adjoint - adjoint * growth).astype(jnp.bfloat16)
                coupled[p, 64 + lo : 64 + hi, 128:256] = (
                    adjoint - adjoint * (growth / ratio)
                ).astype(jnp.bfloat16)
        return carry

    lax.fori_loop(0, half // FAR_UNROLL, far_build, 0)

    image = apply(0, u_wait, mom_wait)
    ff, fw = total(first * first), total(first * image)
    c1 = safe(fw, ff)
    left_over = image - c1 * first
    ff, fw, c1, rr, fr = exchange(1, [ff, fw, c1, total(left_over * left_over), total(first * left_over)])
    h11 = add(fw) / entries
    d1 = c1 - h11
    h21 = jnp.sqrt(jnp.maximum(add(rr + 2.0 * d1 * fr + d1 * d1 * ff), 0.0) / entries + eps)
    second = (image - h11 * first) / h21
    second_ref[...] = second
    wide_u[1, :, pl.ds(clusters, clusters), :] = second
    u_wait, mom_wait = send_density(1)

    image = apply(1, u_wait, mom_wait)
    ff, fv, vv = total(first * first), total(first * second), total(second * second)
    fw, vw = total(first * image), total(second * image)
    c1 = safe(fw, ff)
    left_over = image - c1 * first
    c2 = safe(total(second * left_over), vv)
    left_over = left_over - c2 * second
    ff, fv, vv, fw, vw, c1, c2, rr, fr, vr = exchange(
        2,
        [ff, fv, vv, fw, vw, c1, c2]
        + [total(x * left_over) for x in (left_over, first, second)],
    )
    h12, h22 = add(fw) / entries, add(vw) / entries
    d1, d2 = c1 - h12, c2 - h22
    length_sq = add(rr + 2.0 * (d1 * fr + d2 * vr) + d1 * d1 * ff + 2.0 * d1 * d2 * fv + d2 * d2 * vv)
    h32 = jnp.sqrt(jnp.maximum(length_sq, 0.0) / entries + eps)
    third_ref[...] = (image - h12 * first - h22 * second) / h32
    out = jnp.zeros((8, 128), jnp.float32)
    for index, value in enumerate((h11, h21, h12, h22, h32)):
        out = jnp.where(lane8 == index, value, out)
    hess_ref[...] = out


def shards(rhs, geometry, proxies, basis_in, basis_out, far_tasks, near_tiles):
    clusters = basis_in.shape[0]
    rank = basis_in.shape[2]
    panels = geometry.shape[1]
    members = panels // clusters
    n = lax.axis_size("rows")
    total_clusters = clusters * n
    first_cluster = lax.axis_index("rows") * clusters
    near_local = (near_tiles - first_cluster + clusters) % total_clusters
    near_count = near_tiles.shape[0]
    tasks = far_tasks.shape[1]
    width = -(-tasks // 128) * 128

    geo = features(geometry).reshape(8, clusters, members)
    geo_row = jnp.transpose(geo, (1, 0, 2))
    geo_col = jnp.transpose(geo, (1, 2, 0))
    proxy = jnp.transpose(features(proxies).reshape(8, clusters // 2, 2 * rank), (1, 0, 2))
    task_rows = jnp.pad(far_tasks[0:1], ((0, 7), (0, width - tasks)), constant_values=-1)

    f32, bf16 = jnp.float32, jnp.bfloat16
    vmem = pl.BlockSpec(memory_space=pltpu.VMEM)
    smem = pl.BlockSpec(memory_space=pltpu.SMEM)
    second, third, hess = pl.pallas_call(
        functools.partial(kernel, n),
        out_shape=(
            jax.ShapeDtypeStruct((2, clusters, members), f32),
            jax.ShapeDtypeStruct((2, clusters, members), f32),
            jax.ShapeDtypeStruct((8, 128), f32),
        ),
        in_specs=[smem, smem] + [vmem] * 7,
        out_specs=(vmem, vmem, vmem),
        scratch_shapes=[
            pltpu.VMEM((3 * clusters, 8, members), f32),
            pltpu.VMEM((total_clusters // 2, 8, 2 * rank), f32),
            pltpu.VMEM((clusters * near_count, 2, members, 2 * members), f32),
            pltpu.VMEM((tasks // 2, 2 * rank, 4 * rank), bf16),
            pltpu.VMEM((2, 2, 3 * clusters, members), f32),
            pltpu.VMEM((2, total_clusters, 2 * rank), f32),
            pltpu.VMEM((width, 2 * rank), f32),
            pltpu.VMEM((2, total_clusters, 2 * rank), f32),
            pltpu.VMEM((2, n, clusters, 2 * rank), f32),
            pltpu.VMEM((3, 16, 128), f32),
            pltpu.VMEM((3, n, 16, 128), f32),
            pltpu.VMEM((2, clusters, members), f32),
            pltpu.VMEM((2, clusters, members), f32),
            pltpu.VMEM((2, tasks // 2, 2 * rank), f32),
            pltpu.VMEM((clusters, 2 * rank), f32),
            pltpu.VMEM((48, 896), bf16),
            pltpu.SemaphoreType.DMA((8, n)),
            pltpu.SemaphoreType.DMA((8, n)),
            pltpu.SemaphoreType.DMA((3, 2)),
            pltpu.SemaphoreType.DMA((3, 2)),
        ],
        compiler_params=pltpu.CompilerParams(
            collective_id=0, has_side_effects=True, vmem_limit_bytes=48 * 1024 * 1024
        ),
    )(
        near_local,
        far_tasks,
        rhs.reshape(2, clusters, members),
        geo_row,
        geo_col,
        proxy,
        basis_in.reshape(clusters, 2 * rank, members),
        basis_out.reshape(clusters, 2 * rank, members),
        task_rows,
    )
    return (second.reshape(2, panels), third.reshape(2, panels), hess[0, :5])


def solution(mesh):
    return jax.shard_map(
        shards,
        mesh=mesh,
        in_specs=(
            P(None, ("groups", "rows")),
            P(None, ("groups", "rows")),
            P(None, ("groups", "rows")),
            P(("groups", "rows"), None, None, None),
            P(("groups", "rows"), None, None, None),
            P(None, ("groups", "rows")),
            P(None, ("groups", "rows")),
        ),
        out_specs=(P(None, ("groups", "rows")), P(None, ("groups", "rows")), P("groups")),
        check_vma=False,
    )
```

```python
import functools

import jax
import jax.numpy as jnp
from jax import lax
from jax.experimental import pallas as pl
from jax.experimental.pallas import tpu as pltpu
from jax.sharding import PartitionSpec as P

coulomb = 1.0 / (4.0 * 3.141592653589793)
kappa = 0.5
ratio = 4.0
eps = 1e-06
MESH = pl.DeviceIdType.MESH

FAR_UNROLL = 8
FAR_CHUNK = 32
NEAR_CHUNK = 32
TERM_UNROLL = 16
UNROLL = 1

PROXY, NORM, MOMENT, EXPAND, DOTS = 0, 1, 2, 4, 6


def features(points):
    polar, azimuth = points[3], points[4]
    return jnp.stack(
        [
            points[0],
            points[1],
            points[2],
            jnp.sin(polar) * jnp.cos(azimuth),
            jnp.sin(polar) * jnp.sin(azimuth),
            jnp.cos(polar),
            points[5],
            jnp.zeros_like(points[0]),
        ]
    )


def pair_terms(target, source):
    dx, dy, dz = target[0] - source[0], target[1] - source[1], target[2] - source[2]
    dist_sq = dx * dx + dy * dy + dz * dz + target[6] + source[6]
    inverse = lax.rsqrt(dist_sq)
    radius = dist_sq * inverse
    screen = jnp.exp(-kappa * radius)
    growth = (1.0 + kappa * radius) * screen
    single = (coulomb * source[6]) * inverse
    cube = single * (inverse * inverse)
    double = cube * (dx * source[3] + dy * source[4] + dz * source[5])
    adjoint = -cube * (dx * target[3] + dy * target[4] + dz * target[5])
    return single, double, adjoint, screen, growth


def total(x):
    x = jnp.sum(jnp.sum(x, axis=0), axis=0, keepdims=True)
    return jnp.broadcast_to(jnp.sum(x, axis=1, keepdims=True), x.shape)


def pack(values):
    lane = lax.broadcasted_iota(jnp.int32, (1, 128), 1)
    out = jnp.zeros((1, 128), jnp.float32)
    for index, value in enumerate(values):
        out = jnp.where(lane == index, value, out)
    return out


def kernel(
    n,
    near_ref,
    task_ref,
    rhs_ref,
    geo_ref,
    geo_col_hbm,
    proxy_ref,
    basis_in_hbm,
    basis_out_hbm,
    rows_ref,
    second_ref,
    third_ref,
    hess_ref,
    wide_geo,
    all_proxy,
    near_mats,
    coupled,
    wide_u,
    mom_bf,
    mom_all,
    terms,
    exp_send,
    exp_recv,
    dots_send,
    dots_recv,
    near_out,
    far_out,
    pair_out,
    low_exp,
    dots_flat,
    spreader,
    geo_col_ref,
    basis_in_ref,
    basis_out_ref,
    load_sem,
    send_sem,
    recv_sem,
    halo_send,
    halo_recv,
):
    clusters = geo_ref.shape[0]
    pairs = clusters // 2
    tasks = task_ref.shape[1]
    half = tasks // 2
    near_count = near_ref.shape[0]
    entries = 2.0 * clusters * 128 * n
    me = lax.axis_index("rows")
    right, left = lax.rem(me + 1, n), lax.rem(me + n - 1, n)
    peer_of = lambda k: lax.rem(me + k, n)

    loads = [
        pltpu.make_async_copy(src, dst, load_sem.at[i])
        for i, (src, dst) in enumerate(
            (
                (geo_col_hbm, geo_col_ref),
                (basis_in_hbm, basis_in_ref),
                (basis_out_hbm, basis_out_ref),
            )
        )
    ]
    for load in loads:
        load.start()

    barrier = pltpu.get_barrier_semaphore()

    def greet(k, carry):
        pl.semaphore_signal(barrier, inc=1, device_id={"rows": peer_of(k)}, device_id_type=MESH)
        return carry

    lax.fori_loop(1, n, greet, 0)
    pl.semaphore_wait(barrier, n - 1)

    def to_all(phase, src_of, dst):
        def copy(k):
            return pltpu.make_async_remote_copy(
                src_ref=src_of(peer_of(k)),
                dst_ref=dst,
                send_sem=send_sem.at[phase, k],
                recv_sem=recv_sem.at[phase, k],
                device_id={"rows": peer_of(k)},
                device_id_type=MESH,
            )

        def start(k, carry):
            copy(k).start()
            return carry

        def wait(k, carry):
            copy(k).wait()
            return carry

        return (
            lambda: lax.fori_loop(1, n, start, 0, unroll=UNROLL),
            lambda: lax.fori_loop(1, n, wait, 0, unroll=UNROLL),
        )

    def halo(phase, src, at):
        copies = [
            pltpu.make_async_remote_copy(
                src_ref=src,
                dst_ref=at(where),
                send_sem=halo_send.at[phase, side],
                recv_sem=halo_recv.at[phase, side],
                device_id={"rows": device},
                device_id_type=MESH,
            )
            for side, (where, device) in enumerate(((0, right), (2 * clusters, left)))
        ]

        def start():
            for copy in copies:
                copy.start()

        def wait():
            for copy in copies:
                copy.wait()

        return start, wait

    def dots_phase(index):
        return to_all(DOTS - 1 + index if index else NORM, lambda p: dots_send.at[index], dots_recv.at[index, me])

    rhs = rhs_ref[...]
    message = total(rhs * rhs)
    dots_send[0] = message
    norm_start, norm_wait = dots_phase(0)
    norm_start()
    dots_recv[0, me] = message
    geo_start, geo_wait = halo(0, geo_ref, lambda where: wide_geo.at[pl.ds(where, clusters)])
    geo_start()
    wide_geo[pl.ds(clusters, clusters)] = geo_ref[...]
    twin = me + 1 - 2 * lax.rem(me, 2)

    def proxy_copy(src, owner, sem, device):
        return pltpu.make_async_remote_copy(
            src_ref=src,
            dst_ref=all_proxy.at[pl.ds(owner * pairs, pairs)],
            send_sem=send_sem.at[PROXY, sem],
            recv_sem=recv_sem.at[PROXY, sem],
            device_id={"rows": device},
            device_id_type=MESH,
        )

    def proxy_far(k):
        return proxy_copy(proxy_ref, me, 2 * k, peer_of(2 * k))

    def proxy_twin(k):
        owner = lax.rem(me + n - 2 * k, n)
        return proxy_copy(all_proxy.at[pl.ds(owner * pairs, pairs)], owner, 2 * k + 1, twin)

    def proxy_start(k, carry):
        proxy_far(k).start()
        return carry

    def proxy_pass(k, carry):
        proxy_far(k).wait()
        proxy_twin(k).start()
        return carry

    def proxy_wait(k, carry):
        proxy_twin(k).wait()
        return carry

    lax.fori_loop(1, n // 2, proxy_start, 0)
    own_twin = proxy_copy(proxy_ref, me, 1, twin)
    own_twin.start()
    all_proxy[pl.ds(me * pairs, pairs)] = proxy_ref[...]

    lane8 = lax.broadcasted_iota(jnp.int32, (8, 128), 1)
    row8 = lax.broadcasted_iota(jnp.int32, (8, 128), 0)
    upper = lane8 >= 64
    own_row = (lane8 >= 64) == (row8 == 1)

    def send_density(step):
        def moment(c, carry):
            u0 = wide_u[step, 0, pl.ds(clusters + c, 1), :]
            u1 = wide_u[step, 1, pl.ds(clusters + c, 1), :]
            low = jnp.where(row8 == 0, u0, u1).astype(jnp.bfloat16)
            got = lax.dot_general(
                low, basis_in_ref[c], (((1,), (1,)), ((), ())), preferred_element_type=jnp.float32
            )
            got = jnp.where(lane8[:1] < 64, got[0:1], got[1:2])
            low_exp[pl.ds(c, 1), :] = got
            return carry

        u_start, u_wait = halo(
            1 + step,
            wide_u.at[step, :, pl.ds(clusters, clusters)],
            lambda where: wide_u.at[step, :, pl.ds(where, clusters)],
        )
        u_start()
        for c in range(clusters):
            moment(c, 0)
        mom_bf[step, me] = low_exp[...].astype(jnp.bfloat16)
        own = mom_bf.at[step, me]
        mom_start, mom_wait = to_all(MOMENT + step, lambda p: own, own)
        mom_start()
        return u_wait, mom_wait

    def apply(step, u_wait, mom_wait):
        mom_wait()
        mom_all[...] = mom_bf[step].astype(jnp.float32).reshape(mom_all.shape)

        def far_terms(group, carry):
            for q in range(TERM_UNROLL):
                p = group * TERM_UNROLL + q
                picked_a = mom_all[pl.ds(task_ref[1, p], 1), :]
                picked_b = mom_all[pl.ds(task_ref[1, half + p], 1), :]
                low = jnp.where(row8 == 0, picked_a, picked_b).astype(jnp.bfloat16)
                got = jnp.dot(low, coupled[p], preferred_element_type=jnp.float32)
                for k in range(2):
                    block = got[:, k * 128 : k * 128 + 128]
                    pair_out[k, pl.ds(p, 1), :] = jnp.where(upper[:1], block[1:2], block[0:1])
            return carry

        lax.fori_loop(0, half // TERM_UNROLL, far_terms, 0)
        out0, out1 = pair_out[0], pair_out[1]
        below = lax.broadcasted_iota(jnp.int32, out0.shape, 1) < 64
        terms[0:half, :] = jnp.where(below, out0, pltpu.roll(out1, 64, 1))
        terms[half:tasks, :] = jnp.where(below, pltpu.roll(out0, 64, 1), out1)
        term = terms[...]
        high = term.astype(jnp.bfloat16)
        rest = term - high.astype(jnp.float32)
        mid = rest.astype(jnp.bfloat16)
        low = (rest - mid.astype(jnp.float32)).astype(jnp.bfloat16)
        task_rows = rows_ref[0:1, :]
        width = task_rows.shape[1]

        def choose(block, carry):
            start = pl.multiple_of(block * 128, 128)
            wanted = start + lax.broadcasted_iota(jnp.int32, (128, width), 0)
            selector = jnp.where(task_rows == wanted, 1.0, 0.0).astype(jnp.bfloat16)
            dot = lambda part: jnp.dot(selector, part, preferred_element_type=jnp.float32)
            exp_send[step, pl.ds(start, 128), :] = dot(high) + (dot(mid) + dot(low))
            return carry

        lax.fori_loop(0, n * clusters // 128, choose, 0)
        exp_start, exp_wait = to_all(
            EXPAND + step,
            lambda p: exp_send.at[step, pl.ds(p * clusters, clusters)],
            exp_recv.at[step, me],
        )
        exp_start()
        exp_recv[step, me] = exp_send[step, pl.ds(me * clusters, clusters), :]
        u_wait()

        def near_apply(r, carry):
            acc = [jnp.zeros((128, 128), jnp.float32) for _ in range(2)]
            for t in range(near_count):
                b = near_ref[t, r]
                u0 = wide_u[step, 0, pl.ds(b, 1), :]
                u1 = wide_u[step, 1, pl.ds(b, 1), :]
                for k in range(2):
                    acc[k] = acc[k] + (
                        near_mats[r * near_count + t, k, :, 0:128] * u0
                        + near_mats[r * near_count + t, k, :, 128:256] * u1
                    )
            for k in range(2):
                near_out[k, pl.ds(r, 1), :] = jnp.sum(jnp.transpose(acc[k]), axis=0, keepdims=True)
            return carry

        lax.fori_loop(0, clusters, near_apply, 0)
        exp_wait()
        low_exp[...] = jnp.sum(exp_recv[step], axis=0)
        for c in range(clusters):
            row = jnp.where(own_row & (row8 < 2), low_exp[pl.ds(c, 1), :], 0.0).astype(jnp.bfloat16)
            got = jnp.dot(row, basis_out_ref[c], preferred_element_type=jnp.float32)
            far_out[0, pl.ds(c, 1), :] = got[0:1]
            far_out[1, pl.ds(c, 1), :] = got[1:2]
        u = wide_u[step, :, pl.ds(clusters, clusters), :]
        which = lax.broadcasted_iota(jnp.int32, u.shape, 0)
        diag = jnp.where(which == 0, (1.0 + ratio) / 2.0, (1.0 + 1.0 / ratio) / 2.0)
        return diag * u + near_out[...] + far_out[...]

    def safe(top, bottom):
        return jnp.where(bottom > 0.0, top / jnp.where(bottom > 0.0, bottom, 1.0), 0.0)

    def exchange(index, values):
        message = pack(values)
        dots_send[index] = message
        start, wait = dots_phase(index)
        start()
        dots_recv[index, me] = message
        wait()
        dots_flat[...] = dots_recv[index, :, 0, :]
        got = dots_flat[...]
        return [jnp.broadcast_to(got[:, q : q + 1], got.shape) for q in range(len(values))]

    add = lambda x: jnp.sum(x, axis=0, keepdims=True)

    geo_wait()
    for load in loads:
        load.wait()

    def near_build(r, carry):
        sources = [wide_geo[near_ref[t, r]] for t in range(near_count)]
        for lo in range(0, 128, NEAR_CHUNK):
            hi = lo + NEAR_CHUNK
            tcol = [
                jnp.broadcast_to(geo_col_ref[r, lo:hi, c : c + 1], (NEAR_CHUNK, 128)) for c in range(7)
            ]
            for t in range(near_count):
                srow = [sources[t][c : c + 1, :] for c in range(7)]
                single, double, adjoint, screen, growth = pair_terms(tcol, srow)
                at = r * near_count + t
                near_mats[at, 0, lo:hi, 0:128] = double - double * (ratio * growth)
                near_mats[at, 0, lo:hi, 128:256] = single * screen - single
                near_mats[at, 1, lo:hi, 0:128] = adjoint - adjoint * growth
                near_mats[at, 1, lo:hi, 128:256] = adjoint - adjoint * (growth / ratio)
        return carry

    cut = clusters // 2
    lax.fori_loop(0, cut, near_build, 0)
    lax.fori_loop(1, n // 2, proxy_pass, 0)
    norm_wait()
    rhs_sq = add(dots_recv[0, :, 0, :])
    first = rhs / jnp.sqrt(rhs_sq / entries + eps)
    wide_u[0, :, pl.ds(clusters, clusters), :] = first
    u_wait, mom_wait = send_density(0)

    lax.fori_loop(cut, clusters, near_build, 0)

    own_twin.wait()
    lax.fori_loop(1, n // 2, proxy_wait, 0)
    terms[...] = jnp.zeros_like(terms)
    row = lax.broadcasted_iota(jnp.int32, spreader.shape, 0)
    lane = lax.broadcasted_iota(jnp.int32, spreader.shape, 1)
    same = (row % 8 == lane // 128) & (row // 24 == (lane % 128) // 64)
    spreader[...] = jnp.where(same, 1.0, 0.0).astype(jnp.bfloat16)

    def cluster(c):
        both = all_proxy[lax.div(c, 2)]
        return jnp.where(lax.rem(c, 2) == 0, both, pltpu.roll(both, 64, 1))

    def split(x):
        high = x.astype(jnp.bfloat16).astype(jnp.float32)
        mid = (x - high).astype(jnp.bfloat16).astype(jnp.float32)
        return [high, mid, x - high - mid]

    def far_build(group, carry):
        for q in range(FAR_UNROLL):
            p = group * FAR_UNROLL + q
            target = jnp.where(
                upper, pltpu.roll(cluster(task_ref[0, half + p]), 64, 1), cluster(task_ref[0, p])
            )
            parts = split(cluster(task_ref[1, p])) + split(cluster(task_ref[1, half + p]))
            parts = jnp.transpose(jnp.concatenate(parts, axis=0))[0:64].astype(jnp.bfloat16)
            spread = jnp.dot(parts, spreader[...], preferred_element_type=jnp.float32)
            trow = [target[c : c + 1, :] for c in range(7)]
            for lo in range(0, 64, FAR_CHUNK):
                hi = lo + FAR_CHUNK
                scol = [spread[lo:hi, c * 128 : c * 128 + 128] for c in range(7)]
                single, double, adjoint, screen, growth = pair_terms(trow, scol)
                coupled[p, lo:hi, 0:128] = (double - double * (ratio * growth)).astype(jnp.bfloat16)
                coupled[p, 64 + lo : 64 + hi, 0:128] = (single * screen - single).astype(jnp.bfloat16)
                coupled[p, lo:hi, 128:256] = (adjoint - adjoint * growth).astype(jnp.bfloat16)
                coupled[p, 64 + lo : 64 + hi, 128:256] = (
                    adjoint - adjoint * (growth / ratio)
                ).astype(jnp.bfloat16)
        return carry

    lax.fori_loop(0, half // FAR_UNROLL, far_build, 0)

    image = apply(0, u_wait, mom_wait)
    ff, fw = total(first * first), total(first * image)
    c1 = safe(fw, ff)
    left_over = image - c1 * first
    ff, fw, c1, rr, fr = exchange(1, [ff, fw, c1, total(left_over * left_over), total(first * left_over)])
    h11 = add(fw) / entries
    d1 = c1 - h11
    h21 = jnp.sqrt(jnp.maximum(add(rr + 2.0 * d1 * fr + d1 * d1 * ff), 0.0) / entries + eps)
    second = (image - h11 * first) / h21
    second_ref[...] = second
    wide_u[1, :, pl.ds(clusters, clusters), :] = second
    u_wait, mom_wait = send_density(1)

    image = apply(1, u_wait, mom_wait)
    ff, fv, vv = total(first * first), total(first * second), total(second * second)
    fw, vw = total(first * image), total(second * image)
    c1 = safe(fw, ff)
    left_over = image - c1 * first
    c2 = safe(total(second * left_over), vv)
    left_over = left_over - c2 * second
    ff, fv, vv, fw, vw, c1, c2, rr, fr, vr = exchange(
        2,
        [ff, fv, vv, fw, vw, c1, c2]
        + [total(x * left_over) for x in (left_over, first, second)],
    )
    h12, h22 = add(fw) / entries, add(vw) / entries
    d1, d2 = c1 - h12, c2 - h22
    length_sq = add(rr + 2.0 * (d1 * fr + d2 * vr) + d1 * d1 * ff + 2.0 * d1 * d2 * fv + d2 * d2 * vv)
    h32 = jnp.sqrt(jnp.maximum(length_sq, 0.0) / entries + eps)
    third_ref[...] = (image - h12 * first - h22 * second) / h32
    out = jnp.zeros((8, 128), jnp.float32)
    for index, value in enumerate((h11, h21, h12, h22, h32)):
        out = jnp.where(lane8 == index, value, out)
    hess_ref[...] = out


def shards(rhs, geometry, proxies, basis_in, basis_out, far_tasks, near_tiles):
    clusters = basis_in.shape[0]
    rank = basis_in.shape[2]
    panels = geometry.shape[1]
    members = panels // clusters
    n = lax.axis_size("rows")
    total_clusters = clusters * n
    first_cluster = lax.axis_index("rows") * clusters
    near_local = (near_tiles - first_cluster + clusters) % total_clusters
    near_count = near_tiles.shape[0]
    tasks = far_tasks.shape[1]
    width = -(-tasks // 128) * 128

    geo = features(geometry).reshape(8, clusters, members)
    geo_row = jnp.transpose(geo, (1, 0, 2))
    geo_col = jnp.transpose(geo, (1, 2, 0))
    proxy = jnp.transpose(features(proxies).reshape(8, clusters // 2, 2 * rank), (1, 0, 2))
    task_rows = jnp.pad(far_tasks[0:1], ((0, 7), (0, width - tasks)), constant_values=-1)

    f32, bf16 = jnp.float32, jnp.bfloat16
    vmem = pl.BlockSpec(memory_space=pltpu.VMEM)
    smem = pl.BlockSpec(memory_space=pltpu.SMEM)
    hbm = pl.BlockSpec(memory_space=pl.ANY)
    second, third, hess = pl.pallas_call(
        functools.partial(kernel, n),
        out_shape=(
            jax.ShapeDtypeStruct((2, clusters, members), f32),
            jax.ShapeDtypeStruct((2, clusters, members), f32),
            jax.ShapeDtypeStruct((8, 128), f32),
        ),
        in_specs=[smem, smem, vmem, vmem, hbm, vmem, hbm, hbm, vmem],
        out_specs=(vmem, vmem, vmem),
        scratch_shapes=[
            pltpu.VMEM((3 * clusters, 8, members), f32),
            pltpu.VMEM((total_clusters // 2, 8, 2 * rank), f32),
            pltpu.VMEM((clusters * near_count, 2, members, 2 * members), f32),
            pltpu.VMEM((tasks // 2, 2 * rank, 4 * rank), bf16),
            pltpu.VMEM((2, 2, 3 * clusters, members), f32),
            pltpu.VMEM((2, n, clusters, 2 * rank), bf16),
            pltpu.VMEM((total_clusters, 2 * rank), f32),
            pltpu.VMEM((width, 2 * rank), f32),
            pltpu.VMEM((2, total_clusters, 2 * rank), f32),
            pltpu.VMEM((2, n, clusters, 2 * rank), f32),
            pltpu.VMEM((3, 1, 128), f32),
            pltpu.VMEM((3, n, 1, 128), f32),
            pltpu.VMEM((2, clusters, members), f32),
            pltpu.VMEM((2, clusters, members), f32),
            pltpu.VMEM((2, tasks // 2, 2 * rank), f32),
            pltpu.VMEM((clusters, 2 * rank), f32),
            pltpu.VMEM((n, 128), f32),
            pltpu.VMEM((48, 896), bf16),
            pltpu.VMEM((clusters, members, 8), f32),
            pltpu.VMEM((clusters, 2 * rank, members), bf16),
            pltpu.VMEM((clusters, 2 * rank, members), bf16),
            pltpu.SemaphoreType.DMA((3,)),
            pltpu.SemaphoreType.DMA((8, n)),
            pltpu.SemaphoreType.DMA((8, n)),
            pltpu.SemaphoreType.DMA((3, 2)),
            pltpu.SemaphoreType.DMA((3, 2)),
        ],
        compiler_params=pltpu.CompilerParams(
            collective_id=0, has_side_effects=True, vmem_limit_bytes=48 * 1024 * 1024
        ),
    )(
        near_local,
        far_tasks,
        rhs.reshape(2, clusters, members),
        geo_row,
        geo_col,
        proxy,
        basis_in.reshape(clusters, 2 * rank, members),
        basis_out.reshape(clusters, 2 * rank, members),
        task_rows,
    )
    return (second.reshape(2, panels), third.reshape(2, panels), hess[0, :5])


def solution(mesh):
    return jax.shard_map(
        shards,
        mesh=mesh,
        in_specs=(
            P(None, ("groups", "rows")),
            P(None, ("groups", "rows")),
            P(None, ("groups", "rows")),
            P(("groups", "rows"), None, None, None),
            P(("groups", "rows"), None, None, None),
            P(None, ("groups", "rows")),
            P(None, ("groups", "rows")),
        ),
        out_specs=(P(None, ("groups", "rows")), P(None, ("groups", "rows")), P("groups")),
        check_vma=False,
    )
```

```python
import functools

import jax
import jax.numpy as jnp
from jax import lax
from jax.experimental import pallas as pl
from jax.experimental.pallas import tpu as pltpu
from jax.sharding import PartitionSpec as P

coulomb = 1.0 / (4.0 * 3.141592653589793)
kappa = 0.5
ratio = 4.0
eps = 1e-06
MESH = pl.DeviceIdType.MESH

FAR_UNROLL = 16
FAR_CHUNK = 32
NEAR_CHUNK = 16
TERM_UNROLL = 32
UNROLL = 1

PROXY, NORM, MOMENT, EXPAND, DOTS = 0, 1, 2, 4, 6


def features(points):
    polar, azimuth = points[3], points[4]
    return jnp.stack(
        [
            points[0],
            points[1],
            points[2],
            jnp.sin(polar) * jnp.cos(azimuth),
            jnp.sin(polar) * jnp.sin(azimuth),
            jnp.cos(polar),
            points[5],
            jnp.zeros_like(points[0]),
        ]
    )


def pair_terms(target, source):
    dx, dy, dz = target[0] - source[0], target[1] - source[1], target[2] - source[2]
    dist_sq = dx * dx + dy * dy + dz * dz + target[6] + source[6]
    inverse = lax.rsqrt(dist_sq)
    radius = dist_sq * inverse
    screen = jnp.exp(-kappa * radius)
    growth = (1.0 + kappa * radius) * screen
    single = (coulomb * source[6]) * inverse
    cube = single * (inverse * inverse)
    double = cube * (dx * source[3] + dy * source[4] + dz * source[5])
    adjoint = -cube * (dx * target[3] + dy * target[4] + dz * target[5])
    return single, double, adjoint, screen, growth


def total(x):
    x = jnp.sum(jnp.sum(x, axis=0), axis=0, keepdims=True)
    return jnp.broadcast_to(jnp.sum(x, axis=1, keepdims=True), x.shape)


def pack(values):
    lane = lax.broadcasted_iota(jnp.int32, (1, 128), 1)
    out = jnp.zeros((1, 128), jnp.float32)
    for index, value in enumerate(values):
        out = jnp.where(lane == index, value, out)
    return out


def kernel(
    n,
    near_ref,
    task_ref,
    rhs_ref,
    geo_ref,
    geo_col_hbm,
    proxy_ref,
    basis_in_hbm,
    basis_out_hbm,
    rows_ref,
    second_ref,
    third_ref,
    hess_ref,
    wide_geo,
    all_proxy,
    near_mats,
    coupled,
    wide_u,
    mom_bf,
    mom_all,
    terms,
    exp_send,
    exp_recv,
    dots_send,
    dots_recv,
    near_out,
    far_out,
    pair_out,
    low_exp,
    dots_flat,
    spreader,
    geo_col_ref,
    basis_in_ref,
    basis_out_ref,
    load_sem,
    send_sem,
    recv_sem,
    halo_send,
    halo_recv,
):
    clusters = geo_ref.shape[0]
    pairs = clusters // 2
    tasks = task_ref.shape[1]
    half = tasks // 2
    near_count = near_ref.shape[0]
    entries = 2.0 * clusters * 128 * n
    me = lax.axis_index("rows")
    right, left = lax.rem(me + 1, n), lax.rem(me + n - 1, n)
    peer_of = lambda k: lax.rem(me + k, n)

    loads = [
        pltpu.make_async_copy(src, dst, load_sem.at[i])
        for i, (src, dst) in enumerate(
            (
                (geo_col_hbm, geo_col_ref),
                (basis_in_hbm, basis_in_ref),
                (basis_out_hbm, basis_out_ref),
            )
        )
    ]
    for load in loads:
        load.start()

    barrier = pltpu.get_barrier_semaphore()

    def greet(k, carry):
        pl.semaphore_signal(barrier, inc=1, device_id={"rows": peer_of(k)}, device_id_type=MESH)
        return carry

    lax.fori_loop(1, n, greet, 0)
    pl.semaphore_wait(barrier, n - 1)

    def to_all(phase, src_of, dst):
        def copy(k):
            return pltpu.make_async_remote_copy(
                src_ref=src_of(peer_of(k)),
                dst_ref=dst,
                send_sem=send_sem.at[phase, k],
                recv_sem=recv_sem.at[phase, k],
                device_id={"rows": peer_of(k)},
                device_id_type=MESH,
            )

        def start(k, carry):
            copy(k).start()
            return carry

        def wait(k, carry):
            copy(k).wait()
            return carry

        return (
            lambda: lax.fori_loop(1, n, start, 0, unroll=UNROLL),
            lambda: lax.fori_loop(1, n, wait, 0, unroll=UNROLL),
        )

    def halo(phase, src, at):
        copies = [
            pltpu.make_async_remote_copy(
                src_ref=src,
                dst_ref=at(where),
                send_sem=halo_send.at[phase, side],
                recv_sem=halo_recv.at[phase, side],
                device_id={"rows": device},
                device_id_type=MESH,
            )
            for side, (where, device) in enumerate(((0, right), (2 * clusters, left)))
        ]

        def start():
            for copy in copies:
                copy.start()

        def wait():
            for copy in copies:
                copy.wait()

        return start, wait

    def dots_phase(index):
        return to_all(DOTS - 1 + index if index else NORM, lambda p: dots_send.at[index], dots_recv.at[index, me])

    rhs = rhs_ref[...]
    message = total(rhs * rhs)
    dots_send[0] = message
    norm_start, norm_wait = dots_phase(0)
    norm_start()
    dots_recv[0, me] = message
    geo_start, geo_wait = halo(0, geo_ref, lambda where: wide_geo.at[pl.ds(where, clusters)])
    geo_start()
    wide_geo[pl.ds(clusters, clusters)] = geo_ref[...]
    twin = me + 1 - 2 * lax.rem(me, 2)

    def proxy_copy(src, owner, sem, device):
        return pltpu.make_async_remote_copy(
            src_ref=src,
            dst_ref=all_proxy.at[pl.ds(owner * pairs, pairs)],
            send_sem=send_sem.at[PROXY, sem],
            recv_sem=recv_sem.at[PROXY, sem],
            device_id={"rows": device},
            device_id_type=MESH,
        )

    def proxy_far(k):
        return proxy_copy(proxy_ref, me, 2 * k, peer_of(2 * k))

    def proxy_twin(k):
        owner = lax.rem(me + n - 2 * k, n)
        return proxy_copy(all_proxy.at[pl.ds(owner * pairs, pairs)], owner, 2 * k + 1, twin)

    def proxy_start(k, carry):
        proxy_far(k).start()
        return carry

    def proxy_pass(k, carry):
        proxy_far(k).wait()
        proxy_twin(k).start()
        return carry

    def proxy_wait(k, carry):
        proxy_twin(k).wait()
        return carry

    lax.fori_loop(1, n // 2, proxy_start, 0)
    own_twin = proxy_copy(proxy_ref, me, 1, twin)
    own_twin.start()
    all_proxy[pl.ds(me * pairs, pairs)] = proxy_ref[...]

    lane8 = lax.broadcasted_iota(jnp.int32, (8, 128), 1)
    row8 = lax.broadcasted_iota(jnp.int32, (8, 128), 0)
    upper = lane8 >= 64
    own_row = (lane8 >= 64) == (row8 == 1)

    def send_density(step):
        def moment(c, carry):
            u0 = wide_u[step, 0, pl.ds(clusters + c, 1), :]
            u1 = wide_u[step, 1, pl.ds(clusters + c, 1), :]
            low = jnp.where(row8 == 0, u0, u1).astype(jnp.bfloat16)
            got = lax.dot_general(
                low, basis_in_ref[c], (((1,), (1,)), ((), ())), preferred_element_type=jnp.float32
            )
            got = jnp.where(lane8[:1] < 64, got[0:1], got[1:2])
            low_exp[pl.ds(c, 1), :] = got
            return carry

        u_start, u_wait = halo(
            1 + step,
            wide_u.at[step, :, pl.ds(clusters, clusters)],
            lambda where: wide_u.at[step, :, pl.ds(where, clusters)],
        )
        u_start()
        for c in range(clusters):
            moment(c, 0)
        mom_bf[step, me] = low_exp[...].astype(jnp.bfloat16)
        own = mom_bf.at[step, me]
        mom_start, mom_wait = to_all(MOMENT + step, lambda p: own, own)
        mom_start()
        return u_wait, mom_wait

    def apply(step, u_wait, mom_wait):
        mom_wait()
        mom_all[...] = mom_bf[step].astype(jnp.float32).reshape(mom_all.shape)

        def far_terms(group, carry):
            for q in range(TERM_UNROLL):
                p = group * TERM_UNROLL + q
                picked_a = mom_all[pl.ds(task_ref[1, p], 1), :]
                picked_b = mom_all[pl.ds(task_ref[1, half + p], 1), :]
                low = jnp.where(row8 == 0, picked_a, picked_b).astype(jnp.bfloat16)
                got = jnp.dot(low, coupled[p], preferred_element_type=jnp.float32)
                for k in range(2):
                    block = got[:, k * 128 : k * 128 + 128]
                    pair_out[k, pl.ds(p, 1), :] = jnp.where(upper[:1], block[1:2], block[0:1])
            return carry

        lax.fori_loop(0, half // TERM_UNROLL, far_terms, 0)
        out0, out1 = pair_out[0], pair_out[1]
        below = lax.broadcasted_iota(jnp.int32, out0.shape, 1) < 64
        terms[0:half, :] = jnp.where(below, out0, pltpu.roll(out1, 64, 1))
        terms[half:tasks, :] = jnp.where(below, pltpu.roll(out0, 64, 1), out1)
        term = terms[...]
        high = term.astype(jnp.bfloat16)
        rest = term - high.astype(jnp.float32)
        mid = rest.astype(jnp.bfloat16)
        low = (rest - mid.astype(jnp.float32)).astype(jnp.bfloat16)
        task_rows = rows_ref[0:1, :]
        width = task_rows.shape[1]

        def choose(block, carry):
            start = pl.multiple_of(block * 128, 128)
            wanted = start + lax.broadcasted_iota(jnp.int32, (128, width), 0)
            selector = jnp.where(task_rows == wanted, 1.0, 0.0).astype(jnp.bfloat16)
            dot = lambda part: jnp.dot(selector, part, preferred_element_type=jnp.float32)
            exp_send[step, pl.ds(start, 128), :] = dot(high) + (dot(mid) + dot(low))
            return carry

        lax.fori_loop(0, n * clusters // 128, choose, 0)
        exp_start, exp_wait = to_all(
            EXPAND + step,
            lambda p: exp_send.at[step, pl.ds(p * clusters, clusters)],
            exp_recv.at[step, me],
        )
        exp_start()
        exp_recv[step, me] = exp_send[step, pl.ds(me * clusters, clusters), :]
        u_wait()

        def near_apply(r, carry):
            acc = [jnp.zeros((128, 128), jnp.float32) for _ in range(2)]
            for t in range(near_count):
                b = near_ref[t, r]
                u0 = wide_u[step, 0, pl.ds(b, 1), :]
                u1 = wide_u[step, 1, pl.ds(b, 1), :]
                for k in range(2):
                    acc[k] = acc[k] + (
                        near_mats[r * near_count + t, k, :, 0:128] * u0
                        + near_mats[r * near_count + t, k, :, 128:256] * u1
                    )
            for k in range(2):
                near_out[k, pl.ds(r, 1), :] = jnp.sum(jnp.transpose(acc[k]), axis=0, keepdims=True)
            return carry

        lax.fori_loop(0, clusters, near_apply, 0)
        exp_wait()
        low_exp[...] = jnp.sum(exp_recv[step], axis=0)
        for c in range(clusters):
            row = jnp.where(own_row & (row8 < 2), low_exp[pl.ds(c, 1), :], 0.0).astype(jnp.bfloat16)
            got = jnp.dot(row, basis_out_ref[c], preferred_element_type=jnp.float32)
            far_out[0, pl.ds(c, 1), :] = got[0:1]
            far_out[1, pl.ds(c, 1), :] = got[1:2]
        u = wide_u[step, :, pl.ds(clusters, clusters), :]
        which = lax.broadcasted_iota(jnp.int32, u.shape, 0)
        diag = jnp.where(which == 0, (1.0 + ratio) / 2.0, (1.0 + 1.0 / ratio) / 2.0)
        return diag * u + near_out[...] + far_out[...]

    def safe(top, bottom):
        return jnp.where(bottom > 0.0, top / jnp.where(bottom > 0.0, bottom, 1.0), 0.0)

    def exchange(index, values):
        message = pack(values)
        dots_send[index] = message
        start, wait = dots_phase(index)
        start()
        dots_recv[index, me] = message
        wait()
        dots_flat[...] = dots_recv[index, :, 0, :]
        got = dots_flat[...]
        return [jnp.broadcast_to(got[:, q : q + 1], got.shape) for q in range(len(values))]

    add = lambda x: jnp.sum(x, axis=0, keepdims=True)

    geo_wait()
    for load in loads:
        load.wait()

    def near_build(r, carry):
        sources = [wide_geo[near_ref[t, r]] for t in range(near_count)]
        for lo in range(0, 128, NEAR_CHUNK):
            hi = lo + NEAR_CHUNK
            tcol = [
                jnp.broadcast_to(geo_col_ref[r, lo:hi, c : c + 1], (NEAR_CHUNK, 128)) for c in range(7)
            ]
            for t in range(near_count):
                srow = [sources[t][c : c + 1, :] for c in range(7)]
                single, double, adjoint, screen, growth = pair_terms(tcol, srow)
                at = r * near_count + t
                near_mats[at, 0, lo:hi, 0:128] = double - double * (ratio * growth)
                near_mats[at, 0, lo:hi, 128:256] = single * screen - single
                near_mats[at, 1, lo:hi, 0:128] = adjoint - adjoint * growth
                near_mats[at, 1, lo:hi, 128:256] = adjoint - adjoint * (growth / ratio)
        return carry

    cut = clusters // 2
    lax.fori_loop(0, cut, near_build, 0)
    lax.fori_loop(1, n // 2, proxy_pass, 0)
    norm_wait()
    rhs_sq = add(dots_recv[0, :, 0, :])
    first = rhs / jnp.sqrt(rhs_sq / entries + eps)
    wide_u[0, :, pl.ds(clusters, clusters), :] = first
    u_wait, mom_wait = send_density(0)

    lax.fori_loop(cut, clusters, near_build, 0)

    own_twin.wait()
    lax.fori_loop(1, n // 2, proxy_wait, 0)
    terms[...] = jnp.zeros_like(terms)
    row = lax.broadcasted_iota(jnp.int32, spreader.shape, 0)
    lane = lax.broadcasted_iota(jnp.int32, spreader.shape, 1)
    same = (row % 8 == lane // 128) & (row // 24 == (lane % 128) // 64)
    spreader[...] = jnp.where(same, 1.0, 0.0).astype(jnp.bfloat16)

    def cluster(c):
        both = all_proxy[lax.div(c, 2)]
        return jnp.where(lax.rem(c, 2) == 0, both, pltpu.roll(both, 64, 1))

    def split(x):
        high = x.astype(jnp.bfloat16).astype(jnp.float32)
        mid = (x - high).astype(jnp.bfloat16).astype(jnp.float32)
        return [high, mid, x - high - mid]

    def far_build(group, carry):
        for q in range(FAR_UNROLL):
            p = group * FAR_UNROLL + q
            target = jnp.where(
                upper, pltpu.roll(cluster(task_ref[0, half + p]), 64, 1), cluster(task_ref[0, p])
            )
            parts = split(cluster(task_ref[1, p])) + split(cluster(task_ref[1, half + p]))
            parts = jnp.transpose(jnp.concatenate(parts, axis=0))[0:64].astype(jnp.bfloat16)
            spread = jnp.dot(parts, spreader[...], preferred_element_type=jnp.float32)
            trow = [target[c : c + 1, :] for c in range(7)]
            for lo in range(0, 64, FAR_CHUNK):
                hi = lo + FAR_CHUNK
                scol = [spread[lo:hi, c * 128 : c * 128 + 128] for c in range(7)]
                single, double, adjoint, screen, growth = pair_terms(trow, scol)
                coupled[p, lo:hi, 0:128] = (double - double * (ratio * growth)).astype(jnp.bfloat16)
                coupled[p, 64 + lo : 64 + hi, 0:128] = (single * screen - single).astype(jnp.bfloat16)
                coupled[p, lo:hi, 128:256] = (adjoint - adjoint * growth).astype(jnp.bfloat16)
                coupled[p, 64 + lo : 64 + hi, 128:256] = (
                    adjoint - adjoint * (growth / ratio)
                ).astype(jnp.bfloat16)
        return carry

    lax.fori_loop(0, half // FAR_UNROLL, far_build, 0)

    ff = total(first * first)
    image = apply(0, u_wait, mom_wait)
    fw = total(first * image)
    c1 = safe(fw, ff)
    left_over = image - c1 * first
    ff, fw, c1, rr, fr = exchange(1, [ff, fw, c1, total(left_over * left_over), total(first * left_over)])
    h11 = add(fw) / entries
    d1 = c1 - h11
    h21 = jnp.sqrt(jnp.maximum(add(rr + 2.0 * d1 * fr + d1 * d1 * ff), 0.0) / entries + eps)
    second = (image - h11 * first) / h21
    second_ref[...] = second
    wide_u[1, :, pl.ds(clusters, clusters), :] = second
    u_wait, mom_wait = send_density(1)

    ff, fv, vv = total(first * first), total(first * second), total(second * second)
    image = apply(1, u_wait, mom_wait)
    fw, vw = total(first * image), total(second * image)
    c1 = safe(fw, ff)
    left_over = image - c1 * first
    c2 = safe(total(second * left_over), vv)
    left_over = left_over - c2 * second
    ff, fv, vv, fw, vw, c1, c2, rr, fr, vr = exchange(
        2,
        [ff, fv, vv, fw, vw, c1, c2]
        + [total(x * left_over) for x in (left_over, first, second)],
    )
    h12, h22 = add(fw) / entries, add(vw) / entries
    d1, d2 = c1 - h12, c2 - h22
    length_sq = add(rr + 2.0 * (d1 * fr + d2 * vr) + d1 * d1 * ff + 2.0 * d1 * d2 * fv + d2 * d2 * vv)
    h32 = jnp.sqrt(jnp.maximum(length_sq, 0.0) / entries + eps)
    third_ref[...] = (image - h12 * first - h22 * second) / h32
    out = jnp.zeros((8, 128), jnp.float32)
    for index, value in enumerate((h11, h21, h12, h22, h32)):
        out = jnp.where(lane8 == index, value, out)
    hess_ref[...] = out


def shards(rhs, geometry, proxies, basis_in, basis_out, far_tasks, near_tiles):
    clusters = basis_in.shape[0]
    rank = basis_in.shape[2]
    panels = geometry.shape[1]
    members = panels // clusters
    n = lax.axis_size("rows")
    total_clusters = clusters * n
    first_cluster = lax.axis_index("rows") * clusters
    near_local = (near_tiles - first_cluster + clusters) % total_clusters
    near_count = near_tiles.shape[0]
    tasks = far_tasks.shape[1]
    width = -(-tasks // 128) * 128

    geo = features(geometry).reshape(8, clusters, members)
    geo_row = jnp.transpose(geo, (1, 0, 2))
    geo_col = jnp.transpose(geo, (1, 2, 0))
    proxy = jnp.transpose(features(proxies).reshape(8, clusters // 2, 2 * rank), (1, 0, 2))
    task_rows = jnp.pad(far_tasks[0:1], ((0, 7), (0, width - tasks)), constant_values=-1)

    f32, bf16 = jnp.float32, jnp.bfloat16
    vmem = pl.BlockSpec(memory_space=pltpu.VMEM)
    smem = pl.BlockSpec(memory_space=pltpu.SMEM)
    hbm = pl.BlockSpec(memory_space=pl.ANY)
    second, third, hess = pl.pallas_call(
        functools.partial(kernel, n),
        out_shape=(
            jax.ShapeDtypeStruct((2, clusters, members), f32),
            jax.ShapeDtypeStruct((2, clusters, members), f32),
            jax.ShapeDtypeStruct((8, 128), f32),
        ),
        in_specs=[smem, smem, vmem, vmem, hbm, vmem, hbm, hbm, vmem],
        out_specs=(vmem, vmem, vmem),
        scratch_shapes=[
            pltpu.VMEM((3 * clusters, 8, members), f32),
            pltpu.VMEM((total_clusters // 2, 8, 2 * rank), f32),
            pltpu.VMEM((clusters * near_count, 2, members, 2 * members), f32),
            pltpu.VMEM((tasks // 2, 2 * rank, 4 * rank), bf16),
            pltpu.VMEM((2, 2, 3 * clusters, members), f32),
            pltpu.VMEM((2, n, clusters, 2 * rank), bf16),
            pltpu.VMEM((total_clusters, 2 * rank), f32),
            pltpu.VMEM((width, 2 * rank), f32),
            pltpu.VMEM((2, total_clusters, 2 * rank), f32),
            pltpu.VMEM((2, n, clusters, 2 * rank), f32),
            pltpu.VMEM((3, 1, 128), f32),
            pltpu.VMEM((3, n, 1, 128), f32),
            pltpu.VMEM((2, clusters, members), f32),
            pltpu.VMEM((2, clusters, members), f32),
            pltpu.VMEM((2, tasks // 2, 2 * rank), f32),
            pltpu.VMEM((clusters, 2 * rank), f32),
            pltpu.VMEM((n, 128), f32),
            pltpu.VMEM((48, 896), bf16),
            pltpu.VMEM((clusters, members, 8), f32),
            pltpu.VMEM((clusters, 2 * rank, members), bf16),
            pltpu.VMEM((clusters, 2 * rank, members), bf16),
            pltpu.SemaphoreType.DMA((3,)),
            pltpu.SemaphoreType.DMA((8, n)),
            pltpu.SemaphoreType.DMA((8, n)),
            pltpu.SemaphoreType.DMA((3, 2)),
            pltpu.SemaphoreType.DMA((3, 2)),
        ],
        compiler_params=pltpu.CompilerParams(
            collective_id=0, has_side_effects=True, vmem_limit_bytes=48 * 1024 * 1024
        ),
    )(
        near_local,
        far_tasks,
        rhs.reshape(2, clusters, members),
        geo_row,
        geo_col,
        proxy,
        basis_in.reshape(clusters, 2 * rank, members),
        basis_out.reshape(clusters, 2 * rank, members),
        task_rows,
    )
    return (second.reshape(2, panels), third.reshape(2, panels), hess[0, :5])


def solution(mesh):
    return jax.shard_map(
        shards,
        mesh=mesh,
        in_specs=(
            P(None, ("groups", "rows")),
            P(None, ("groups", "rows")),
            P(None, ("groups", "rows")),
            P(("groups", "rows"), None, None, None),
            P(("groups", "rows"), None, None, None),
            P(None, ("groups", "rows")),
            P(None, ("groups", "rows")),
        ),
        out_specs=(P(None, ("groups", "rows")), P(None, ("groups", "rows")), P("groups")),
        check_vma=False,
    )
```
